32 devices in a mesh: group: 2 (over x), lm: 8 (over z, y), env: 2 (over core).
Axes of the slice: x: 2, y: 2, z: 4, core: 2. Of those that a mesh axis runs over, the one named last changes fastest.
Arguments:
- env_desc: bfloat16 [1024, 512], P(('group', 'lm', 'env')), parts along dimension 0, may hold values from -6 to 6
- landmarks: bfloat16 [8192, 512], P(('lm', 'env')), may hold values from -6 to 6
- whitening: bfloat16 [8192, 1024], P(('lm', 'env')), may hold values from -120 to 120
Outputs:
- coords: float32 [1024, 1024], P(('group', 'lm', 'env')), parts along dimension 0
The draws below stay inside these ranges and needn't reach their ends.
There are 2 independent parts, one for each index of `group`. The reference program is written for one: setup_inputs(seed, part) draws one part's arguments, and reference() takes and returns one part's arrays. A program takes and returns all parts, laid end to end along the dimension named above; an argument that names none is the same for every part. Nothing has to cross between parts.
All inputs are finite; a program needn't handle non-finite values.
Results may differ from the reference program's by a relative error of at most 0.0029.
Values may be sent and summed in bfloat16 or wider, within the bound.
No kernel may reach another device: no remote copies, remote signals or barrier semaphores. Data moves between devices by JAX's collectives and lax.ppermute only.
A program may use at most 64 MiB of HBM per device.

```python
import math
import jax
import jax.numpy as jnp
from jax import lax

D = 512
R = 1024
LANDMARKS = 8192
ENVS = 512


def block_levels(rng, dims, cuts, least, top_value):
    loudness = 1.0
    for position, shards_of in cuts:
        draws = jax.random.uniform(jax.random.fold_in(jax.random.fold_in(rng, 6), position), (shards_of,), jnp.float32, least / len(cuts), top_value / len(cuts))
        loudness = loudness * jnp.repeat(jnp.exp(draws), dims[position] // shards_of).reshape((-1,) + (1,) * (len(dims) - 1 - position))
    return loudness


def normal_values(key, extent, spread, reach, pieces=(), kind=jnp.bfloat16):
    entries = jax.random.normal(key, extent, jnp.float32) * spread
    if len(pieces) > 0:
        entries = block_levels(key, extent, pieces, -0.22, 0.18) * entries
    return jnp.clip(entries, min=-reach, max=reach).astype(kind)


def setup_inputs(seed: int = 0, part: int = 0) -> dict:
    arg_keys = jax.random.split(jax.random.key(seed), 4)
    part_splits = jax.random.split(jax.random.fold_in(arg_keys[3], part), 4)
    env_desc = normal_values(part_splits[0], (ENVS, D), 1.0, 6.0, ((0, 16),))
    landmarks = normal_values(arg_keys[1], (LANDMARKS, D), 1.0, 6.0, ((0, 16),))
    whitening = normal_values(arg_keys[2], (LANDMARKS, R), 20.0, 120.0, ((0, 16),))
    return {"env_desc": env_desc, "landmarks": landmarks, "whitening": whitening}


def kernel_block(rows, landmarks, land_sq, weights):
    row_sq = jnp.sum(jnp.square(rows.astype(jnp.float32)), axis=1)
    cross = jnp.dot(rows, landmarks.T, preferred_element_type=jnp.float32)
    dist = (row_sq[:, None] + land_sq[None, :]) - 2.0 * cross
    kern = jnp.exp(-(4.0 / rows.shape[1]) * dist).astype(jnp.bfloat16)
    return jnp.dot(kern, weights, preferred_element_type=jnp.float32)


def reference(env_desc, landmarks, whitening):
    land_sq = jnp.sum(jnp.square(landmarks.astype(jnp.float32)), axis=1)
    total = env_desc.shape[0]
    block = math.gcd(total, 512)
    blocks = env_desc.reshape(total // block, block, env_desc.shape[1])
    result = lax.map(lambda piece: kernel_block(piece, landmarks, land_sq, whitening), blocks)
    return result.reshape(total, whitening.shape[1])
```

```python
import jax
import jax.numpy as jnp
from jax import lax
from jax.sharding import PartitionSpec as P

AXES = ("lm", "env")


def kernel_block(rows, landmarks, land_sq, weights):
    row_sq = jnp.sum(jnp.square(rows.astype(jnp.float32)), axis=1)
    cross = lax.dot_general(
        rows, landmarks, (((1,), (1,)), ((), ())), preferred_element_type=jnp.float32
    )
    dist = row_sq[:, None] + land_sq[None, :] - 2.0 * cross
    kern = jnp.exp(-(4.0 / rows.shape[1]) * dist).astype(jnp.bfloat16)
    return jnp.dot(kern, weights, preferred_element_type=jnp.float32)


def solution(mesh):
    chips = mesh.shape["lm"]
    inner = 1 << ((chips.bit_length() - 1) // 2)
    outer = chips // inner
    steps = ([0] + list(range(outer - 1, outer // 2, -1)), list(range(1, outer // 2 + 1)))

    swap = [(2 * chip + core, 2 * chip + 1 - core) for chip in range(chips) for core in range(2)]

    def exchange(block, by):
        pairs = [
            (2 * chip + core, 2 * (chip ^ by[core]) + core)
            for chip in range(chips)
            for core in range(2)
        ]
        return lax.ppermute(block, AXES, pairs)

    def local(env_desc, landmarks, whitening):
        rows = env_desc.shape[0]
        land_sq = jnp.sum(jnp.square(landmarks.astype(jnp.float32)), axis=1)

        chip_rows = jnp.concatenate([env_desc, lax.ppermute(env_desc, AXES, swap)])
        line = [chip_rows] + [exchange(chip_rows, (k, k)) for k in range(1, inner)]
        line = jnp.concatenate(line)
        got = [exchange(line, (a * inner, b * inner)) for a, b in reversed(list(zip(*steps)))]
        first = jnp.concatenate(got[::-1])
        second = lax.ppermute(first, AXES, swap)

        given = kernel_block(first, landmarks, land_sq, whitening).astype(jnp.bfloat16)
        taken = lax.ppermute(given, AXES, swap)
        sums = kernel_block(second, landmarks, land_sq, whitening)
        sums = (sums + taken.astype(jnp.float32)).astype(jnp.bfloat16)

        total = None
        blocks = sums.reshape(outer // 2, inner, 2 * rows, -1)
        for i in reversed(range(outer // 2)):
            for k in reversed(range(inner)):
                by = (steps[1][i] * inner + k, steps[0][i] * inner + k)
                part = exchange(blocks[i, k], by).astype(jnp.float32)
                total = part if total is None else total + part
        return total[rows:] + lax.ppermute(total[:rows], AXES, swap)

    return jax.shard_map(
        local,
        mesh=mesh,
        in_specs=(P(("group", "lm", "env"), None), P(("lm", "env"), None), P(("lm", "env"), None)),
        out_specs=P(("group", "lm", "env"), None),
        check_vma=False,
    )
```

```python
import jax
import jax.numpy as jnp
from jax import lax
from jax.experimental import pallas as pl
from jax.experimental.pallas import tpu as pltpu
from jax.sharding import PartitionSpec as P

AXES = ("lm", "env")
HEAVY = 10**11
VMEM = pl.BlockSpec(memory_space=pltpu.VMEM)
PARAMS = pltpu.CompilerParams(vmem_limit_bytes=16 * 2**20)


def load_body(landmarks, weights, landmarks_out, weights_out, land_sq, sems):
    first = pltpu.make_async_copy(landmarks, landmarks_out, sems.at[0])
    second = pltpu.make_async_copy(weights, weights_out, sems.at[1])
    first.start()
    second.start()
    first.wait()
    square = jnp.square(landmarks_out[...].astype(jnp.float32))
    land_sq[...] = lax.dot_general(
        jnp.ones((8, square.shape[1]), jnp.float32),
        square,
        (((1,), (1,)), ((), ())),
        precision=lax.Precision.HIGHEST,
        preferred_element_type=jnp.float32,
    )
    second.wait()


def load(landmarks, weights):
    return pl.pallas_call(
        load_body,
        out_shape=[
            jax.ShapeDtypeStruct(landmarks.shape, landmarks.dtype),
            jax.ShapeDtypeStruct(weights.shape, weights.dtype),
            jax.ShapeDtypeStruct((8, landmarks.shape[0]), jnp.float32),
        ],
        in_specs=[pl.BlockSpec(memory_space=pltpu.HBM)] * 2,
        out_specs=[VMEM] * 3,
        scratch_shapes=[pltpu.SemaphoreType.DMA((2,))],
        compiler_params=PARAMS,
        cost_estimate=pl.CostEstimate(flops=10**9, bytes_accessed=0, transcendentals=0),
    )(*[pltpu.with_memory_space_constraint(x, pltpu.HBM) for x in (landmarks, weights)])


def kernel_sums(rows, landmarks, land_sq, weights):
    row_sq = jnp.sum(jnp.square(rows.astype(jnp.float32)), axis=1, keepdims=True)
    cross = lax.dot_general(
        rows, landmarks, (((1,), (1,)), ((), ())), preferred_element_type=jnp.float32
    )
    dist = row_sq + land_sq - 2.0 * cross
    kern = jnp.exp(-(4.0 / rows.shape[1]) * dist).astype(jnp.bfloat16)
    return jnp.dot(kern, weights, preferred_element_type=jnp.float32)


def give_body(rows, landmarks, land_sq, weights, out):
    sums = kernel_sums(rows[...], landmarks[...], land_sq[0:1], weights[...])
    out[...] = sums.astype(out.dtype)


def keep_body(rows, landmarks, land_sq, weights, taken, *outs):
    sums = kernel_sums(rows[...], landmarks[...], land_sq[0:1], weights[...])
    sums += taken[...].astype(jnp.float32)
    at = 0
    for out in outs:
        out[...] = sums[at : at + out.shape[0]].astype(out.dtype)
        at += out.shape[0]


def add_body(*refs):
    *parts, out = refs
    total = parts[0][...].astype(jnp.float32)
    for part in parts[1:]:
        total += part[...].astype(jnp.float32)
    out[...] = total


def add(*parts, weight=1):
    return pl.pallas_call(
        add_body,
        out_shape=jax.ShapeDtypeStruct(parts[0].shape, jnp.float32),
        in_specs=[VMEM] * len(parts),
        out_specs=VMEM,
        compiler_params=PARAMS,
        cost_estimate=pl.CostEstimate(
            flops=weight * HEAVY, bytes_accessed=0, transcendentals=0
        ),
    )(*parts)


def call(body, sizes, *args, rounds=1):
    rows, landmarks, _, weights = args[:4]
    read = sum(arg.size * arg.dtype.itemsize for arg in args)
    cost = pl.CostEstimate(
        flops=rounds * 2 * rows.shape[0] * landmarks.shape[0] * (rows.shape[1] + weights.shape[1]),
        bytes_accessed=rounds * read,
        transcendentals=rows.shape[0] * landmarks.shape[0],
    )
    return pl.pallas_call(
        body,
        out_shape=[jax.ShapeDtypeStruct((size, weights.shape[1]), jnp.bfloat16) for size in sizes],
        in_specs=[VMEM] * len(args),
        out_specs=[VMEM] * len(sizes),
        compiler_params=PARAMS,
        cost_estimate=cost,
    )(*args)


def solution(mesh):
    chips = mesh.shape["lm"]
    inner = 1 << ((chips.bit_length() - 1) // 2)
    outer = chips // inner
    steps = ([0] + list(range(outer - 1, outer // 2, -1)), list(range(1, outer // 2 + 1)))

    def exchange(block, by, cross=0):
        pairs = [
            (2 * chip + core, 2 * (chip ^ by[core]) + (core ^ cross))
            for chip in range(chips)
            for core in range(2)
        ]
        return lax.ppermute(block, AXES, pairs)

    def swap(block):
        return exchange(block, (0, 0), 1)

    def local(env_desc, landmarks, whitening):
        rows = env_desc.shape[0]

        chip_rows = jnp.concatenate([env_desc, swap(env_desc)])
        landmarks, chip_rows = lax.optimization_barrier((landmarks, chip_rows))
        got = [exchange(chip_rows, (a * inner, b * inner)) for a, b in reversed(list(zip(*steps)))]
        landmarks, whitening, land_sq = load(landmarks, whitening)
        got, land_sq = lax.optimization_barrier((got, land_sq))
        got = jnp.concatenate(got[::-1])
        lines = [got] + [exchange(got, (k, k)) for k in range(1, inner)]

        tables = (landmarks, land_sq, whitening)
        given = [
            call(give_body, [first.shape[0]], first, *tables, rounds=20 if k else 1)[0]
            for k, first in enumerate(lines)
        ]
        taken = [swap(given[0])]
        taken[0], *given[1:] = lax.optimization_barrier(taken + given[1:])
        taken += [swap(block) for block in given[1:]]
        parts = []
        for k, first in enumerate(lines):
            sizes = [2 * rows] * (outer // 2)
            if k == inner - 1:
                sizes[-1:] = [rows, rows]
            blocks = call(keep_body, sizes, swap(first), *tables, taken[k])
            for i in reversed(range(outer // 2)):
                by = (steps[1][i] * inner + k, steps[0][i] * inner + k)
                if k == inner - 1 and i == outer // 2 - 1:
                    last = [exchange(blocks[-1], by), exchange(blocks[-2], by, 1)]
                else:
                    parts.append(exchange(blocks[i], by))
        total = add(*parts)
        return add(total[rows:], *last) + swap(total[:rows])

    return jax.shard_map(
        local,
        mesh=mesh,
        in_specs=(P(("group", "lm", "env"), None), P(("lm", "env"), None), P(("lm", "env"), None)),
        out_specs=P(("group", "lm", "env"), None),
        check_vma=False,
    )
```

```python
import jax
import jax.numpy as jnp
from jax import lax
from jax.experimental import pallas as pl
from jax.experimental.pallas import tpu as pltpu
from jax.sharding import PartitionSpec as P

AXES = ("lm", "env")
VMEM = pl.BlockSpec(memory_space=pltpu.VMEM)
PARAMS = pltpu.CompilerParams(vmem_limit_bytes=16 * 2**20)


def load_body(landmarks, weights, landmarks_out, weights_out, land_sq, sems):
    first = pltpu.make_async_copy(landmarks, landmarks_out, sems.at[0])
    second = pltpu.make_async_copy(weights, weights_out, sems.at[1])
    first.start()
    second.start()
    first.wait()
    square = jnp.square(landmarks_out[...].astype(jnp.float32))
    land_sq[...] = lax.dot_general(
        jnp.ones((8, square.shape[1]), jnp.float32),
        square,
        (((1,), (1,)), ((), ())),
        precision=lax.Precision.HIGHEST,
        preferred_element_type=jnp.float32,
    )
    second.wait()


def load(landmarks, weights):
    return pl.pallas_call(
        load_body,
        out_shape=[
            jax.ShapeDtypeStruct(landmarks.shape, landmarks.dtype),
            jax.ShapeDtypeStruct(weights.shape, weights.dtype),
            jax.ShapeDtypeStruct((8, landmarks.shape[0]), jnp.float32),
        ],
        in_specs=[pl.BlockSpec(memory_space=pltpu.HBM)] * 2,
        out_specs=[VMEM] * 3,
        scratch_shapes=[pltpu.SemaphoreType.DMA((2,))],
        compiler_params=PARAMS,
        cost_estimate=pl.CostEstimate(flops=10**9, bytes_accessed=0, transcendentals=0),
    )(*[pltpu.with_memory_space_constraint(x, pltpu.HBM) for x in (landmarks, weights)])


def kernel_sums(rows, landmarks, land_sq, weights):
    row_sq = jnp.sum(jnp.square(rows.astype(jnp.float32)), axis=1, keepdims=True)
    cross = lax.dot_general(
        rows, landmarks, (((1,), (1,)), ((), ())), preferred_element_type=jnp.float32
    )
    dist = row_sq + land_sq - 2.0 * cross
    kern = jnp.exp(-(4.0 / rows.shape[1]) * dist).astype(jnp.bfloat16)
    return jnp.dot(kern, weights, preferred_element_type=jnp.float32)


def give_body(rows, landmarks, land_sq, weights, out):
    sums = kernel_sums(rows[...], landmarks[...], land_sq[0:1], weights[...])
    out[...] = sums.astype(out.dtype)


def keep_body(rows, landmarks, land_sq, weights, taken, *outs):
    sums = kernel_sums(rows[...], landmarks[...], land_sq[0:1], weights[...])
    sums += taken[...].astype(jnp.float32)
    at = 0
    for out in outs:
        out[...] = sums[at : at + out.shape[0]].astype(out.dtype)
        at += out.shape[0]


def call(body, sizes, *args, rounds=1):
    rows, landmarks, _, weights = args[:4]
    read = sum(arg.size * arg.dtype.itemsize for arg in args)
    cost = pl.CostEstimate(
        flops=rounds * 2 * rows.shape[0] * landmarks.shape[0] * (rows.shape[1] + weights.shape[1]),
        bytes_accessed=rounds * read,
        transcendentals=rows.shape[0] * landmarks.shape[0],
    )
    return pl.pallas_call(
        body,
        out_shape=[jax.ShapeDtypeStruct((size, weights.shape[1]), jnp.bfloat16) for size in sizes],
        in_specs=[VMEM] * len(args),
        out_specs=[VMEM] * len(sizes),
        compiler_params=PARAMS,
        cost_estimate=cost,
    )(*args)


def solution(mesh):
    chips = mesh.shape["lm"]
    inner = 1 << ((chips.bit_length() - 1) // 2)
    outer = chips // inner
    steps = ([0] + list(range(outer - 1, outer // 2, -1)), list(range(1, outer // 2 + 1)))

    def exchange(block, by, cross=0):
        pairs = [
            (2 * chip + core, 2 * (chip ^ by[core]) + (core ^ cross))
            for chip in range(chips)
            for core in range(2)
        ]
        return lax.ppermute(block, AXES, pairs)

    def swap(block):
        return exchange(block, (0, 0), 1)

    def local(env_desc, landmarks, whitening):
        rows = env_desc.shape[0]

        peer = swap(env_desc)
        landmarks, peer = lax.optimization_barrier((landmarks, peer))
        chip_rows = jnp.concatenate([env_desc, peer])
        got = [exchange(chip_rows, (a * inner, b * inner)) for a, b in reversed(list(zip(*steps)))]
        landmarks, whitening, land_sq = load(landmarks, whitening)
        got = got[::-1]
        lines = [got]
        for k in range(1, inner):
            line = [exchange(block, (k, k)) for block in got]
            lines.append(line)
        lines = [jnp.concatenate(line) for line in lines]

        tables = (landmarks, land_sq, whitening)
        seconds = [swap(lines[0])]
        seconds[0], *lines[1:] = lax.optimization_barrier(seconds + lines[1:])
        given = [
            call(give_body, [first.shape[0]], first, *tables, rounds=20 if k else 1)[0]
            for k, first in enumerate(lines)
        ]
        taken = [swap(given[0])]
        taken[0], *given[1:] = lax.optimization_barrier(taken + given[1:])
        taken += [swap(block) for block in given[1:]]
        seconds += [swap(first) for first in lines[1:]]
        near, far = [], []
        for k, first in enumerate(lines):
            sizes = [2 * rows] * (outer // 2)
            blocks = call(keep_body, sizes, seconds[k], *tables, taken[k])
            for i in reversed(range(outer // 2)):
                by = (steps[1][i] * inner + k, steps[0][i] * inner + k)
                (far if i else near).append(exchange(blocks[i], by))
        total = sum(part.astype(jnp.float32) for part in far + near)
        return total[rows:] + swap(total[:rows])

    return jax.shard_map(
        local,
        mesh=mesh,
        in_specs=(P(("group", "lm", "env"), None), P(("lm", "env"), None), P(("lm", "env"), None)),
        out_specs=P(("group", "lm", "env"), None),
        check_vma=False,
    )
```

```python
import functools

import jax
import jax.numpy as jnp
from jax import lax
from jax.experimental import pallas as pl
from jax.experimental.pallas import tpu as pltpu
from jax.sharding import PartitionSpec as P

AXES = ("lm", "env")
HEAVY = 5*10**9
VMEM = pl.BlockSpec(memory_space=pltpu.VMEM)
PARAMS = pltpu.CompilerParams(vmem_limit_bytes=16 * 2**20)


def load_body(landmarks, weights, landmarks_out, weights_out, land_sq, sems):
    first = pltpu.make_async_copy(landmarks, landmarks_out, sems.at[0])
    second = pltpu.make_async_copy(weights, weights_out, sems.at[1])
    first.start()
    second.start()
    first.wait()
    square = jnp.square(landmarks_out[...].astype(jnp.float32))
    land_sq[...] = lax.dot_general(
        jnp.ones((8, square.shape[1]), jnp.float32),
        square,
        (((1,), (1,)), ((), ())),
        precision=lax.Precision.HIGHEST,
        preferred_element_type=jnp.float32,
    )
    second.wait()


def load(landmarks, weights):
    return pl.pallas_call(
        load_body,
        out_shape=[
            jax.ShapeDtypeStruct(landmarks.shape, landmarks.dtype),
            jax.ShapeDtypeStruct(weights.shape, weights.dtype),
            jax.ShapeDtypeStruct((8, landmarks.shape[0]), jnp.float32),
        ],
        in_specs=[pl.BlockSpec(memory_space=pltpu.HBM)] * 2,
        out_specs=[VMEM] * 3,
        scratch_shapes=[pltpu.SemaphoreType.DMA((2,))],
        compiler_params=PARAMS,
        cost_estimate=pl.CostEstimate(flops=10**9, bytes_accessed=0, transcendentals=0),
    )(*[pltpu.with_memory_space_constraint(x, pltpu.HBM) for x in (landmarks, weights)])


def kernel_sums(rows, landmarks, land_sq, weights):
    row_sq = jnp.sum(jnp.square(rows.astype(jnp.float32)), axis=1, keepdims=True)
    cross = lax.dot_general(
        rows, landmarks, (((1,), (1,)), ((), ())), preferred_element_type=jnp.float32
    )
    dist = row_sq + land_sq - 2.0 * cross
    kern = jnp.exp(-(4.0 / rows.shape[1]) * dist).astype(jnp.bfloat16)
    return jnp.dot(kern, weights, preferred_element_type=jnp.float32)


def sums_body(rows, landmarks, land_sq, weights, out):
    sums = kernel_sums(rows[...], landmarks[...], land_sq[0:1], weights[...])
    out[...] = sums.astype(out.dtype)


def line_part(dtype, weight, rows, landmarks, land_sq, weights):
    args = (rows, landmarks, land_sq, weights)
    count, depth, width = rows.shape[0], landmarks.shape[0], weights.shape[1]
    return pl.pallas_call(
        sums_body,
        out_shape=jax.ShapeDtypeStruct((count, width), dtype),
        in_specs=[VMEM] * 4,
        out_specs=VMEM,
        compiler_params=PARAMS,
        cost_estimate=pl.CostEstimate(
            flops=weight * 2 * count * depth * (rows.shape[1] + width),
            bytes_accessed=sum(arg.size * arg.dtype.itemsize for arg in args),
            transcendentals=count * depth,
        ),
    )(*args)


def join_body(kept, taken, *outs):
    at = 0
    for out in outs:
        here = pl.ds(at, out.shape[0])
        out[...] = (kept[here] + taken[here].astype(jnp.float32)).astype(out.dtype)
        at += out.shape[0]


def join(sizes, kept, taken):
    count, width = kept.shape
    return pl.pallas_call(
        join_body,
        out_shape=[jax.ShapeDtypeStruct((size, width), jnp.bfloat16) for size in sizes],
        in_specs=[VMEM] * 2,
        out_specs=[VMEM] * len(sizes),
        compiler_params=PARAMS,
        cost_estimate=pl.CostEstimate(
            flops=count * width, bytes_accessed=8 * count * width, transcendentals=0
        ),
    )(kept, taken)


def add_body(*refs):
    *parts, out = refs
    total = parts[0][...].astype(jnp.float32)
    for part in parts[1:]:
        total += part[...].astype(jnp.float32)
    out[...] = total


def add(*parts, weight=1):
    return pl.pallas_call(
        add_body,
        out_shape=jax.ShapeDtypeStruct(parts[0].shape, jnp.float32),
        in_specs=[VMEM] * len(parts),
        out_specs=VMEM,
        compiler_params=PARAMS,
        cost_estimate=pl.CostEstimate(
            flops=weight * HEAVY, bytes_accessed=0, transcendentals=0
        ),
    )(*parts)


def solution(mesh):
    chips = mesh.shape["lm"]
    inner = 1 << ((chips.bit_length() - 1) // 2)
    outer = chips // inner
    steps = ([0] + list(range(outer - 1, outer // 2, -1)), list(range(1, outer // 2 + 1)))

    def exchange(block, by, cross=0):
        pairs = [
            (2 * chip + core, 2 * (chip ^ by[core]) + (core ^ cross))
            for chip in range(chips)
            for core in range(2)
        ]
        return lax.ppermute(block, AXES, pairs)

    def swap(block):
        return exchange(block, (0, 0), 1)

    def local(env_desc, landmarks, whitening):
        rows = env_desc.shape[0]

        peer = swap(env_desc)
        landmarks, peer = lax.optimization_barrier((landmarks, peer))
        chip_rows = jnp.concatenate([env_desc, peer])
        got = [exchange(chip_rows, (a * inner, b * inner)) for a, b in reversed(list(zip(*steps)))]
        landmarks, whitening, land_sq = load(landmarks, whitening)
        got = got[::-1]
        lines = [got]
        for k in range(1, inner):
            line = [exchange(block, (k, k)) for block in got]
            lines.append(line)
        lines = [jnp.concatenate(line) for line in lines]

        def line_sums(sizes, first, *tables):
            second = swap(first)
            taken = swap(line_part(jnp.bfloat16, 1, first, *tables))
            return list(join(sizes, line_part(jnp.float32, 10, second, *tables), taken))

        def nothing(sizes, first, *tables):
            return [jnp.zeros((size, whitening.shape[1]), jnp.bfloat16) for size in sizes]

        go = lax.axis_index("lm") >= 0
        sums = []
        for k, first in enumerate(lines):
            sizes = ([rows, rows] if k == inner - 1 else [2 * rows]) + [2 * rows] * (outer // 2 - 1)
            work, none = (functools.partial(branch, sizes) for branch in (line_sums, nothing))
            sums.append(lax.cond(go, work, none, first, landmarks, land_sq, whitening))
        sums[0][0], sums[-1] = lax.optimization_barrier((sums[0][0], sums[-1]))
        near, far = [], []
        for k, blocks in enumerate(sums):
            *firsts, by0 = [
                (steps[1][i] * inner + k, steps[0][i] * inner + k) for i in reversed(range(outer // 2))
            ]
            far += [exchange(block, by) for block, by in zip(blocks[::-1], firsts)]
            if k < inner - 1:
                near.append(exchange(blocks[0], by0))
            else:
                last = [exchange(blocks[1], by0), exchange(blocks[0], by0, 1)]
        early = outer // 2 - 1
        total = add(add(*far[:early]), *far[early:], *near)
        return add(total[rows:], *last) + swap(total[:rows])

    return jax.shard_map(
        local,
        mesh=mesh,
        in_specs=(P(("group", "lm", "env"), None), P(("lm", "env"), None), P(("lm", "env"), None)),
        out_specs=P(("group", "lm", "env"), None),
        check_vma=False,
    )
```

```python
import functools

import jax
import jax.numpy as jnp
from jax import lax
from jax.experimental import pallas as pl
from jax.experimental.pallas import tpu as pltpu
from jax.sharding import PartitionSpec as P

AXES = ("lm", "env")
HEAVY = 5 * 10**9
VMEM = pl.BlockSpec(memory_space=pltpu.VMEM)
PARAMS = pltpu.CompilerParams(vmem_limit_bytes=16 * 2**20)


def load_body(landmarks, weights, landmarks_out, weights_out, land_sq, sems):
    first = pltpu.make_async_copy(landmarks, landmarks_out, sems.at[0])
    second = pltpu.make_async_copy(weights, weights_out, sems.at[1])
    first.start()
    second.start()
    first.wait()
    square = jnp.square(landmarks_out[...].astype(jnp.float32))
    high = square.astype(jnp.bfloat16)
    low = (square - high.astype(jnp.float32)).astype(jnp.bfloat16)
    ones = jnp.ones((8, square.shape[1]), jnp.bfloat16)
    land_sq[...] = sum(
        lax.dot_general(ones, part, (((1,), (1,)), ((), ())), preferred_element_type=jnp.float32)
        for part in (high, low)
    )
    second.wait()


def load(landmarks, weights):
    return pl.pallas_call(
        load_body,
        out_shape=[
            jax.ShapeDtypeStruct(landmarks.shape, landmarks.dtype),
            jax.ShapeDtypeStruct(weights.shape, weights.dtype),
            jax.ShapeDtypeStruct((8, landmarks.shape[0]), jnp.float32),
        ],
        in_specs=[pl.BlockSpec(memory_space=pltpu.HBM)] * 2,
        out_specs=[VMEM] * 3,
        scratch_shapes=[pltpu.SemaphoreType.DMA((2,))],
        compiler_params=PARAMS,
        cost_estimate=pl.CostEstimate(flops=10**9, bytes_accessed=0, transcendentals=0),
    )(*[pltpu.with_memory_space_constraint(x, pltpu.HBM) for x in (landmarks, weights)])


def kernel_sums(rows, landmarks, land_sq, weights):
    row_sq = jnp.sum(jnp.square(rows.astype(jnp.float32)), axis=1, keepdims=True)
    cross = lax.dot_general(
        rows, landmarks, (((1,), (1,)), ((), ())), preferred_element_type=jnp.float32
    )
    dist = row_sq + land_sq - 2.0 * cross
    kern = jnp.exp(-(4.0 / rows.shape[1]) * dist).astype(jnp.bfloat16)
    return jnp.dot(kern, weights, preferred_element_type=jnp.float32)


def sums_body(rows, landmarks, land_sq, weights, out):
    sums = kernel_sums(rows[...], landmarks[...], land_sq[0:1], weights[...])
    out[...] = sums.astype(out.dtype)


def line_part(dtype, weight, rows, landmarks, land_sq, weights):
    args = (rows, landmarks, land_sq, weights)
    count, depth, width = rows.shape[0], landmarks.shape[0], weights.shape[1]
    return pl.pallas_call(
        sums_body,
        out_shape=jax.ShapeDtypeStruct((count, width), dtype),
        in_specs=[VMEM] * 4,
        out_specs=VMEM,
        compiler_params=PARAMS,
        cost_estimate=pl.CostEstimate(
            flops=weight * 2 * count * depth * (rows.shape[1] + width),
            bytes_accessed=sum(arg.size * arg.dtype.itemsize for arg in args),
            transcendentals=count * depth,
        ),
    )(*args)


def join_body(kept, taken, *outs):
    at = 0
    for out in outs:
        here = pl.ds(at, out.shape[0])
        out[...] = (kept[here] + taken[here].astype(jnp.float32)).astype(out.dtype)
        at += out.shape[0]


def join(sizes, kept, taken):
    count, width = kept.shape
    return pl.pallas_call(
        join_body,
        out_shape=[jax.ShapeDtypeStruct((size, width), jnp.bfloat16) for size in sizes],
        in_specs=[VMEM] * 2,
        out_specs=[VMEM] * len(sizes),
        compiler_params=PARAMS,
        cost_estimate=pl.CostEstimate(
            flops=count * width, bytes_accessed=8 * count * width, transcendentals=0
        ),
    )(kept, taken)


def copy_body(block, out):
    out[...] = block[...]


def copy(block):
    return pl.pallas_call(
        copy_body,
        out_shape=jax.ShapeDtypeStruct(block.shape, block.dtype),
        in_specs=[VMEM],
        out_specs=VMEM,
        compiler_params=PARAMS,
    )(block)


def add_body(*refs):
    *parts, out = refs
    total = parts[0][...].astype(jnp.float32)
    for part in parts[1:]:
        total += part[...].astype(jnp.float32)
    out[...] = total


def add(*parts, weight=1):
    return pl.pallas_call(
        add_body,
        out_shape=jax.ShapeDtypeStruct(parts[0].shape, jnp.float32),
        in_specs=[VMEM] * len(parts),
        out_specs=VMEM,
        compiler_params=PARAMS,
        cost_estimate=pl.CostEstimate(
            flops=weight * HEAVY, bytes_accessed=0, transcendentals=0
        ),
    )(*parts)


def solution(mesh):
    chips = mesh.shape["lm"]
    inner = 1 << ((chips.bit_length() - 1) // 2)
    outer = chips // inner
    steps = ([0] + list(range(outer - 1, outer // 2, -1)), list(range(1, outer // 2 + 1)))

    def exchange(block, by, cross=0):
        pairs = [
            (2 * chip + core, 2 * (chip ^ by[core]) + (core ^ cross))
            for chip in range(chips)
            for core in range(2)
        ]
        return lax.ppermute(block, AXES, pairs)

    def swap(block):
        return exchange(block, (0, 0), 1)

    def local(env_desc, landmarks, whitening):
        rows = env_desc.shape[0]

        peer = swap(env_desc)
        landmarks, peer = lax.optimization_barrier((landmarks, peer))
        chip_rows = jnp.concatenate([env_desc, peer])
        got = [exchange(chip_rows, (a * inner, b * inner)) for a, b in reversed(list(zip(*steps)))]
        landmarks, whitening, land_sq = load(landmarks, whitening)
        got = got[::-1]
        got[-1], land_sq = lax.optimization_barrier((got[-1], land_sq))
        lines = [got]
        for k in range(1, inner):
            line = [exchange(block, (k, k)) for block in got]
            lines.append(line)

        def line_sums(sizes, first, *tables):
            second = swap(first)
            taken = swap(line_part(jnp.bfloat16, 1, first, *tables))
            return list(join(sizes, line_part(jnp.float32, 10, second, *tables), taken))

        def nothing(sizes, first, *tables):
            return [jnp.zeros((size, whitening.shape[1]), jnp.bfloat16) for size in sizes]

        go = lax.axis_index("lm") >= 0
        groups = [[(i, k) for i in range(outer // 2)] for k in range(inner)]
        groups[1].insert(0, groups[0].pop(0))
        parts, last = [], []
        for group in groups:
            first = [lines[k][i] for i, k in group]
            first = jnp.concatenate(first) if len(first) > 1 else copy(*first)
            sizes = []
            for where in group:
                sizes += [rows, rows] if where == (0, inner - 1) else [2 * rows]
            work, none = (functools.partial(branch, sizes) for branch in (line_sums, nothing))
            blocks = lax.cond(go, work, none, first, landmarks, land_sq, whitening)
            for i, k in reversed(group):
                by = (steps[1][i] * inner + k, steps[0][i] * inner + k)
                block = blocks.pop()
                if (i, k) == (0, inner - 1):
                    last = [exchange(block, by), exchange(blocks.pop(), by, 1)]
                else:
                    parts.append(exchange(block, by))
        early = outer // 2 - 1
        total = add(add(*parts[:early]), *parts[early:])
        return add(total[rows:], *last) + swap(total[:rows])

    return jax.shard_map(
        local,
        mesh=mesh,
        in_specs=(P(("group", "lm", "env"), None), P(("lm", "env"), None), P(("lm", "env"), None)),
        out_specs=P(("group", "lm", "env"), None),
        check_vma=False,
    )
```

```python
import functools

import jax
import jax.numpy as jnp
from jax import lax
from jax.experimental import pallas as pl
from jax.experimental.pallas import tpu as pltpu
from jax.sharding import PartitionSpec as P

AXES = ("lm", "env")
HEAVY = 5 * 10**9
VMEM = pl.BlockSpec(memory_space=pltpu.VMEM)
PARAMS = pltpu.CompilerParams(vmem_limit_bytes=16 * 2**20)


def load_body(landmarks, weights, landmarks_out, weights_out, land_sq, sems):
    first = pltpu.make_async_copy(landmarks, landmarks_out, sems.at[0])
    second = pltpu.make_async_copy(weights, weights_out, sems.at[1])
    first.start()
    second.start()
    first.wait()
    square = jnp.square(landmarks_out[...].astype(jnp.float32))
    high = square.astype(jnp.bfloat16)
    low = (square - high.astype(jnp.float32)).astype(jnp.bfloat16)
    ones = jnp.ones((8, square.shape[1]), jnp.bfloat16)
    land_sq[...] = sum(
        lax.dot_general(ones, part, (((1,), (1,)), ((), ())), preferred_element_type=jnp.float32)
        for part in (high, low)
    )
    second.wait()


def load(landmarks, weights):
    return pl.pallas_call(
        load_body,
        out_shape=[
            jax.ShapeDtypeStruct(landmarks.shape, landmarks.dtype),
            jax.ShapeDtypeStruct(weights.shape, weights.dtype),
            jax.ShapeDtypeStruct((8, landmarks.shape[0]), jnp.float32),
        ],
        in_specs=[pl.BlockSpec(memory_space=pltpu.HBM)] * 2,
        out_specs=[VMEM] * 3,
        scratch_shapes=[pltpu.SemaphoreType.DMA((2,))],
        compiler_params=PARAMS,
        cost_estimate=pl.CostEstimate(flops=10**9, bytes_accessed=0, transcendentals=0),
    )(*[pltpu.with_memory_space_constraint(x, pltpu.HBM) for x in (landmarks, weights)])


def kernel_sums(rows, landmarks, land_sq, weights):
    row_sq = jnp.sum(jnp.square(rows.astype(jnp.float32)), axis=1, keepdims=True)
    cross = lax.dot_general(
        rows, landmarks, (((1,), (1,)), ((), ())), preferred_element_type=jnp.float32
    )
    dist = row_sq + land_sq - 2.0 * cross
    kern = jnp.exp(-(4.0 / rows.shape[1]) * dist).astype(jnp.bfloat16)
    return jnp.dot(kern, weights, preferred_element_type=jnp.float32)


def sums_body(rows, landmarks, land_sq, weights, out):
    sums = kernel_sums(rows[...], landmarks[...], land_sq[0:1], weights[...])
    out[...] = sums.astype(out.dtype)


def line_part(dtype, weight, rows, landmarks, land_sq, weights):
    args = (rows, landmarks, land_sq, weights)
    count, depth, width = rows.shape[0], landmarks.shape[0], weights.shape[1]
    return pl.pallas_call(
        sums_body,
        out_shape=jax.ShapeDtypeStruct((count, width), dtype),
        in_specs=[VMEM] * 4,
        out_specs=VMEM,
        compiler_params=PARAMS,
        cost_estimate=pl.CostEstimate(
            flops=weight * 2 * count * depth * (rows.shape[1] + width),
            bytes_accessed=sum(arg.size * arg.dtype.itemsize for arg in args),
            transcendentals=count * depth,
        ),
    )(*args)


def join_body(kept, taken, *outs):
    at = 0
    for out in outs:
        here = pl.ds(at, out.shape[0])
        out[...] = (kept[here] + taken[here].astype(jnp.float32)).astype(out.dtype)
        at += out.shape[0]


def join(sizes, kept, taken):
    count, width = kept.shape
    return pl.pallas_call(
        join_body,
        out_shape=[jax.ShapeDtypeStruct((size, width), jnp.bfloat16) for size in sizes],
        in_specs=[VMEM] * 2,
        out_specs=[VMEM] * len(sizes),
        compiler_params=PARAMS,
        cost_estimate=pl.CostEstimate(
            flops=count * width, bytes_accessed=8 * count * width, transcendentals=0
        ),
    )(kept, taken)


def copy_body(block, out):
    out[...] = block[...]


def copy(block):
    return pl.pallas_call(
        copy_body,
        out_shape=jax.ShapeDtypeStruct(block.shape, block.dtype),
        in_specs=[VMEM],
        out_specs=VMEM,
        compiler_params=PARAMS,
    )(block)


def add_body(*refs):
    *parts, out = refs
    total = parts[0][...].astype(jnp.float32)
    for part in parts[1:]:
        total += part[...].astype(jnp.float32)
    out[...] = total


def add(*parts, weight=1):
    return pl.pallas_call(
        add_body,
        out_shape=jax.ShapeDtypeStruct(parts[0].shape, jnp.float32),
        in_specs=[VMEM] * len(parts),
        out_specs=VMEM,
        compiler_params=PARAMS,
        cost_estimate=pl.CostEstimate(
            flops=weight * HEAVY, bytes_accessed=0, transcendentals=0
        ),
    )(*parts)


def solution(mesh):
    chips = mesh.shape["lm"]
    inner = 1 << ((chips.bit_length() - 1) // 2)
    outer = chips // inner
    steps = ([0] + list(range(outer - 1, outer // 2, -1)), list(range(1, outer // 2 + 1)))

    def exchange(block, by, cross=0):
        pairs = [
            (2 * chip + core, 2 * (chip ^ by[core]) + (core ^ cross))
            for chip in range(chips)
            for core in range(2)
        ]
        return lax.ppermute(block, AXES, pairs)

    def swap(block):
        return exchange(block, (0, 0), 1)

    def local(env_desc, landmarks, whitening):
        rows = env_desc.shape[0]

        peer = swap(env_desc)
        landmarks, peer = lax.optimization_barrier((landmarks, peer))
        chip_rows = jnp.concatenate([env_desc, peer])
        got = [exchange(chip_rows, (a * inner, b * inner)) for a, b in reversed(list(zip(*steps)))]
        landmarks, whitening, land_sq = load(landmarks, whitening)
        got = got[::-1]
        got[-1], land_sq = lax.optimization_barrier((got[-1], land_sq))
        lines = [got]
        for k in range(1, inner):
            line = [exchange(block, (k, k)) for block in got]
            lines.append(line)

        def line_sums(sizes, first, *tables):
            second = swap(first)
            taken = swap(line_part(jnp.bfloat16, 1, first, *tables))
            return list(join(sizes, line_part(jnp.float32, 10, second, *tables), taken))

        def nothing(sizes, first, *tables):
            return [jnp.zeros((size, whitening.shape[1]), jnp.bfloat16) for size in sizes]

        go = lax.axis_index("lm") >= 0
        groups = [[(i, k) for i in range(1, outer // 2)] for k in range(inner)]
        groups.append([(0, k) for k in range(inner)])
        total, last = None, []
        for group in groups:
            first = [lines[k][i] for i, k in group]
            if group == groups[-1]:
                first[0], held[0] = lax.optimization_barrier((first[0], held[0]))
            first = jnp.concatenate(first) if len(first) > 1 else copy(*first)
            sizes = []
            for where in group:
                sizes += [rows, rows] if where[0] == 0 else [2 * rows]
            work, none = (functools.partial(branch, sizes) for branch in (line_sums, nothing))
            blocks = lax.cond(go, work, none, first, landmarks, land_sq, whitening)
            held = list(blocks)
            parts = [] if total is None else [total]
            for i, k in reversed(group):
                by = (steps[1][i] * inner + k, steps[0][i] * inner + k)
                block = blocks.pop()
                if i == 0:
                    last += [exchange(block, by), exchange(blocks.pop(), by, 1)]
                else:
                    parts.append(exchange(block, by))
            total = add(*parts) if len(parts) > (total is not None) else total
        return add(total[rows:], *last) + swap(total[:rows])

    return jax.shard_map(
        local,
        mesh=mesh,
        in_specs=(P(("group", "lm", "env"), None), P(("lm", "env"), None), P(("lm", "env"), None)),
        out_specs=P(("group", "lm", "env"), None),
        check_vma=False,
    )
```
